32 devices in a mesh: chan: 2 (over x), elem: 2 (over y), beam: 8 (over z, core).
Axes of the slice: x: 2, y: 2, z: 4, core: 2. Of those that a mesh axis runs over, the one named last changes fastest.
Arguments:
- voltages: bfloat16 [2, 128, 128, 2048], P(None, 'chan', 'beam', 'elem'), may hold values from -6 to 6
- weights: bfloat16 [2, 128, 2048, 2048], P(None, 'chan', 'elem', 'beam'), may hold values from -0.09375 to 0.09375
Outputs:
- power: float32 [128, 128, 2048], P(None, ('chan', 'elem'), 'beam')
The draws below stay inside these ranges and needn't reach their ends.
All inputs are finite; a program needn't handle non-finite values.
Results may differ from the reference program's by a relative error of at most 0.012.
Values may be sent and summed in bfloat16 or wider, within the bound.
No kernel may reach another device: no remote copies, remote signals or barrier semaphores. Data moves between devices by JAX's collectives and lax.ppermute only.
A program may use at most 192 MiB of HBM per device.

```python
import jax
import jax.numpy as jnp
from jax import lax

C = 128
E = 2048
B = 2048
TIME = 128
N_ELEM = 2


def block_scale(key, extent, split, low, top_value):
    gain = 1.0
    for position, parts in split:
        heights = jax.random.uniform(jax.random.fold_in(jax.random.fold_in(key, 6), position), (parts,), jnp.float32, low / len(split), top_value / len(split))
        gain = gain * jnp.repeat(jnp.exp(heights), extent[position] // parts).reshape((-1,) + (1,) * (len(extent) - 1 - position))
    return gain


def scatter_about(stream_key, shape, spread, limit, cuts=(), held_as=jnp.bfloat16):
    factor_of = block_scale(stream_key, shape, cuts, -0.22, 0.18) if cuts else 1.0
    values = jax.random.normal(stream_key, shape, jnp.float32) * spread * factor_of
    return jnp.minimum(jnp.maximum(values, -limit), limit).astype(held_as)


def setup_inputs(seed: int = 0) -> dict:
    streams_of = jax.random.split(jax.random.key(seed), 3)
    return {
        "voltages": scatter_about(streams_of[0], (2, C, TIME, E), 1.0, 6.0, ((1, 2), (2, 8), (3, 2))),
        "weights": scatter_about(streams_of[1], (2, C, E, B), (2 * E) ** -0.5, 0.09375, ((1, 2), (2, 2), (3, 8))),
    }


def dft_tables(channels):
    index = jnp.arange(channels, dtype=jnp.int32)
    phase = index[:, None] * index[None, :] % channels
    angle = phase.astype(jnp.float32) * (2.0 * jnp.pi / channels)
    factor = 1.0 / jnp.sqrt(jnp.float32(channels))
    return (jnp.cos(angle) * factor, jnp.sin(angle) * factor)

def reference(voltages, weights):
    width = E // N_ELEM
    starts = jnp.arange(N_ELEM, dtype=jnp.int32) * width

    def add_block(running, start):
        volt_block = lax.dynamic_slice_in_dim(voltages, start, width, 3).astype(jnp.float32)
        weight_block = lax.dynamic_slice_in_dim(weights, start, width, 2).astype(jnp.float32)
        real_part = jnp.einsum('cte,ceb->ctb', volt_block[0], weight_block[0]) - jnp.einsum('cte,ceb->ctb', volt_block[1], weight_block[1])
        imag_part = jnp.einsum('cte,ceb->ctb', volt_block[0], weight_block[1]) + jnp.einsum('cte,ceb->ctb', volt_block[1], weight_block[0])
        rounded = jnp.stack([real_part, imag_part]).astype(jnp.bfloat16)
        rounded = lax.optimization_barrier(rounded).astype(jnp.float32)
        return (running + rounded, None)
    initial = jnp.zeros((2, C, TIME, B), jnp.float32)
    summed, unused = lax.scan(add_block, initial, starts)
    beams = lax.optimization_barrier(summed.astype(jnp.bfloat16)).astype(jnp.float32)
    cosine, sine = dft_tables(C)
    real_in = beams[0].reshape(C, TIME * B)
    imag_in = beams[1].reshape(C, TIME * B)
    highest = lax.Precision.HIGHEST
    real_out = jnp.dot(cosine, real_in, precision=highest, preferred_element_type=jnp.float32) - jnp.dot(sine, imag_in, precision=highest, preferred_element_type=jnp.float32)
    imag_out = jnp.dot(sine, real_in, precision=highest, preferred_element_type=jnp.float32) + jnp.dot(cosine, imag_in, precision=highest, preferred_element_type=jnp.float32)
    power = real_out * real_out + imag_out * imag_out
    return power.reshape(C, TIME, B)
```

```python
import functools
import math

import jax
import jax.numpy as jnp
from jax import lax
from jax.experimental import pallas as pl
from jax.experimental.pallas import tpu as pltpu
from jax.sharding import PartitionSpec as P

F32 = jnp.float32
BF16 = jnp.bfloat16
VMEM_BYTES = 40 * 2**20
WINDOW = (3,)
Y_LAG, X_LAG, RING_LAG, UNGATED = 1, 2, 0, 0
FLOPS = 32
CUTS = 2
GROUP = 4
PLAN = ((0, 6), (0, 6), (0, 6), (0, 6), (0, 4), (0, 2), (0, 2))


def groups_of_channels(channels):
    unit = channels // 32
    plan, first = [], 0
    for gathered, units in PLAN:
        plan.append((gathered, first, units * unit))
        first += units * unit
    return plan


def beamform_kernel(sizes, scalars, *refs):
    n, group, time, own, elems, chans, counts, slots = sizes
    halves, refs = refs[: 2 * CUTS], refs[2 * CUTS :]
    blocks, outs = refs[: len(counts)], refs[len(counts) : len(counts) + elems]
    volt, result = refs[len(counts) + elems :]
    step = pl.program_id(0)
    lanes = result.shape[2]
    for g in range(group):
        if blocks[0].shape[2] == time:
            held = blocks[0][:, g].reshape(2 * time, blocks[0].shape[3])
        else:
            slot = 0
            for ref, count in zip(blocks, counts):
                rows = ref.shape[2]
                for j in range(count):
                    at = pl.multiple_of(scalars[slot], rows)
                    volt[g, pl.ds(at, rows), :] = ref[2 * j, g]
                    volt[g, pl.ds(pl.multiple_of(time + at, rows), rows), :] = ref[2 * j + 1, g]
                    slot += 1
            held = volt[g]
        products = []
        for part in range(2):
            total = None
            for j, ref in enumerate(halves[part * CUTS : (part + 1) * CUTS]):
                depth = ref.shape[2]
                term = jnp.dot(held[:, j * depth : (j + 1) * depth], ref[0, g], preferred_element_type=F32)
                total = term if total is None else total + term
            products.append(total)
        by_real, by_imag = products
        real_part = by_real[:time] - by_imag[time:]
        imag_part = by_real[time:] + by_imag[:time]
        row = step * group + g
        for k in range(result.shape[0]):
            cut = slice(k * lanes, (k + 1) * lanes)
            result[k, pl.ds(row, time, stride=2 * n), :] = real_part[:, cut]
            result[k, pl.ds(n + row, time, stride=2 * n), :] = imag_part[:, cut]

    @pl.when(step == n // group - 1)
    def _():
        for r in range(elems):
            for q in range(chans):
                first = pl.multiple_of(scalars[slots + r * chans + q], own) * (2 * n)
                for k in range(result.shape[0]):
                    piece = result[k, pl.ds(pl.multiple_of(first, own * 2 * n), own * 2 * n), :]
                    outs[r][q, :, :, k * lanes : (k + 1) * lanes] = piece.reshape(own, 2 * n, lanes).astype(BF16)


def beamform(scalars, weights, first, n, sources, time, own, elems, chans):
    _, _, depth, beams = weights.shape
    counts = [count for _, count, _ in sources]
    group = math.gcd(math.gcd(first, n), GROUP if n >= 2 * GROUP else GROUP // 2)
    in_specs = [
        pl.BlockSpec(
            (1, group, depth // CUTS, beams), lambda i, s, part=part, j=j: (part, first // group + i, j, 0)
        )
        for part in range(2)
        for j in range(CUTS)
    ]
    for array, count, whole in sources:
        start = first if whole else 0
        in_specs.append(
            pl.BlockSpec((2 * count, group) + array.shape[2:], lambda i, s, start=start: (0, start // group + i, 0, 0))
        )
    shape = (chans, own, 2 * n, beams)
    lanes = min(128, beams)
    return pl.pallas_call(
        functools.partial(beamform_kernel, (n, group, time, own, elems, chans, counts, scalars.shape[0] - elems * chans)),
        out_shape=[jax.ShapeDtypeStruct(shape, BF16)] * elems,
        grid_spec=pltpu.PrefetchScalarGridSpec(
            num_scalar_prefetch=1,
            grid=(n // group,),
            in_specs=in_specs,
            out_specs=[pl.BlockSpec(shape, lambda i, s: (0, 0, 0, 0))] * elems,
            scratch_shapes=[
                pltpu.VMEM((group, 2 * time, depth), BF16),
                pltpu.VMEM((beams // lanes, time * 2 * n, lanes), F32),
            ],
        ),
        compiler_params=pltpu.CompilerParams(vmem_limit_bytes=VMEM_BYTES),
        cost_estimate=pl.CostEstimate(
            flops=FLOPS * n * time * depth * beams,
            bytes_accessed=4 * n * (depth * beams + time * depth + time * beams),
            transcendentals=0,
        ),
        name="beamform",
    )(scalars, *[weights] * (2 * CUTS), *[array for array, _, _ in sources])


def synthesis_kernel(layout, channels, table, *refs):
    out = refs[-1]
    times, beams = out.shape[1], out.shape[2]
    flat = out.reshape(channels * times, beams)
    lanes = min(128, beams)
    for t in range(times):
        rows, at = [], 0
        for elems, chans in layout:
            total = refs[at][0, t].astype(F32)
            for r in range(1, elems):
                total += refs[at + r][0, t].astype(F32)
            rows.append(total)
            at += elems
            for _ in range(1, chans):
                rows.append(refs[at][t].astype(F32))
                at += 1
        held = jnp.concatenate(rows, axis=0).astype(BF16)
        parts = jnp.dot(table[...], held, preferred_element_type=F32)
        half = 2 * channels
        fine = parts[:half] + (parts[half : 2 * half] + parts[2 * half :])
        out[:, t, :] = fine[:channels] * fine[:channels] + fine[channels:] * fine[channels:]


def synthesis(table, groups, channels, own, beams):
    times = 8
    in_specs = [pl.BlockSpec(table.shape, lambda i: (0, 0))]
    operands, layout = [], []
    for partials, received in groups:
        rows = partials[0].shape[2]
        layout.append((len(partials), 1 + len(received)))
        in_specs += [pl.BlockSpec((1, times, rows, beams), lambda i: (0, i, 0, 0))] * len(partials)
        in_specs += [pl.BlockSpec((times, rows, beams), lambda i: (i, 0, 0))] * len(received)
        operands += list(partials) + list(received)
    return pl.pallas_call(
        functools.partial(synthesis_kernel, layout, channels),
        out_shape=jax.ShapeDtypeStruct((channels, own, beams), F32),
        grid=(own // times,),
        in_specs=in_specs,
        out_specs=pl.BlockSpec((channels, times, beams), lambda i: (0, i, 0)),
        compiler_params=pltpu.CompilerParams(vmem_limit_bytes=VMEM_BYTES),
        cost_estimate=pl.CostEstimate(
            flops=24 * channels * channels * own * beams,
            bytes_accessed=channels * own * beams * 12,
            transcendentals=0,
        ),
        name="synthesis",
    )(table, *operands)


def synthesis_table(channels, local, plan, my_chan, chans):
    places, is_imag = [], []
    for _, first, n in plan:
        for q in range(chans):
            base = lax.rem(my_chan + chans - q, chans) * local + first
            place = base + jnp.arange(n, dtype=jnp.int32)
            places += [place, place]
            is_imag += [False] * n + [True] * n
    column = jnp.concatenate(places)
    imag = jnp.array(is_imag)
    index = jnp.arange(channels, dtype=jnp.int32)
    phase = index[:, None] * column[None, :] % channels
    angle = phase.astype(F32) * (2.0 * jnp.pi / channels)
    factor = 1.0 / jnp.sqrt(F32(channels))
    cosine, sine = jnp.cos(angle) * factor, jnp.sin(angle) * factor
    table = jnp.concatenate([jnp.where(imag, -sine, cosine), jnp.where(imag, cosine, sine)])
    high = lax.reduce_precision(table, 8, 7)
    middle = lax.reduce_precision(table - high, 8, 7)
    low = table - high - middle
    return jnp.concatenate([high, middle, low]).astype(BF16)


def after(value, other):
    return lax.optimization_barrier((value, other))[0]


def shards(voltages, weights):
    local, rows = voltages.shape[1], voltages.shape[2]
    beams = weights.shape[3]
    chans, elems, beam_devices = lax.axis_size("chan"), lax.axis_size("elem"), lax.axis_size("beam")
    channels, time = local * chans, rows * beam_devices
    own = time // (chans * elems)
    cores = 2 if beam_devices % 2 == 0 else 1
    chips = beam_devices // cores
    my_chan, my_elem, my_beam = (lax.axis_index(a) for a in ("chan", "elem", "beam"))
    my_chip, my_core = my_beam // cores, my_beam % cores

    ring = [(d, (d + cores) % beam_devices) for d in range(beam_devices)]
    pair = [(d, d ^ 1) for d in range(beam_devices)]
    plan = groups_of_channels(local)

    mate = lax.ppermute(voltages, "beam", pair) if cores == 2 else None
    table = synthesis_table(channels, local, plan, my_chan, chans)

    def offsets(core):
        return [(lax.rem(my_chip + chips - h, chips) * cores + core) * rows for h in range(chips)]

    mine, others = offsets(my_core), offsets(cores - 1 - my_core)
    piece_starts = [
        (lax.rem(my_chan + q, chans) * elems + lax.rem(my_elem + r, elems)) * own
        for r in range(elems)
        for q in range(chans)
    ]
    places = mine + (others if cores == 2 else [])
    scalars = jnp.stack(places + piece_starts).astype(jnp.int32)

    def partial_beams(k, ahead):
        gathered, first, n = plan[k]
        if gathered:
            sources = [(held[k][1], 1, False)]
        else:
            sources = [(voltages, 1, True)] + [(block, 1, False) for block in held[k][1:]]
            if cores == 2:
                sources.append((mate, 1, True))
                if k < len(plan) - 1:
                    swapped = lax.ppermute(jnp.concatenate(held[k][1:]), "beam", pair)
                    sources.append((swapped, chips - 1, False))
                else:
                    sources += [(lax.ppermute(block, "beam", pair), 1, False) for block in held[k][1:]]
        offsets_now = after(scalars, ahead) if ahead else scalars
        return beamform(offsets_now, weights, first, n, sources, time, own, elems, chans)

    def over_elements(partials):
        moved = [
            lax.ppermute(partials[r], "elem", [(d, (d + r) % elems) for d in range(elems)]) for r in range(1, elems)
        ]
        return [partials[0]] + moved

    def sums_to_send(arrived):
        totals = []
        for q in range(1, chans):
            total = arrived[0][q].astype(F32)
            for part in arrived[1:]:
                total = total + part[q].astype(F32)
            totals.append(total.astype(BF16))
        return totals

    def over_channels(totals):
        return [
            lax.ppermute(total, "chan", [(d, (d + q) % chans) for d in range(chans)])
            for q, total in enumerate(totals, 1)
        ]

    ringed = [k for k in range(len(plan)) if not plan[k][0]]
    lead = ringed[0]
    lead_piece = voltages[:, plan[lead][1] : plan[lead][1] + plan[lead][2]]
    later_pieces = after(voltages, lead_piece)
    held = [[later_pieces[:, first : first + n]] for _, first, n in plan]
    held[lead] = [lead_piece]
    for k, (gathered, _, _) in enumerate(plan):
        if gathered:
            held[k].append(lax.all_gather(held[k][0], "beam", axis=2, tiled=True))
    sent, arrived, received = [], [], []
    count = len(ringed)
    partials = []

    def work_on(k):
        ahead = []
        if k < len(plan) - UNGATED:
            if k >= Y_LAG:
                ahead += arrived[k - Y_LAG][1:]
            if k >= X_LAG:
                ahead += received[k - X_LAG]
        partials.append(partial_beams(k, ahead))
        arrived.append(over_elements(partials[k]))
        received.append(over_channels(sums_to_send(arrived[k])))

    for slot in range(count + chips + 1 + RING_LAG):
        waits = []
        if 0 <= slot - chips < count:
            work_on(slot - chips)
        if 0 <= slot - chips - RING_LAG < count:
            waits.append(partials[slot - chips - RING_LAG][-1])
        for h in range(chips - 1):
            if not 0 <= slot - h < count:
                continue
            k = ringed[slot - h]
            block = held[k][h]
            ahead = list(waits) + [sent[-w] for w in WINDOW if len(sent) >= w]
            if ahead:
                block = after(block, ahead)
            got = lax.ppermute(block, "beam", ring)
            held[k].append(got)
            sent.append(got)

    groups = [(arrived[k], received[k]) for k in range(len(plan))]
    return synthesis(table, groups, channels, own, beams)


def solution(mesh):
    placed = (P(None, "chan", "beam", "elem"), P(None, "chan", "elem", "beam"))
    return jax.shard_map(
        shards,
        mesh=mesh,
        in_specs=placed,
        out_specs=P(None, ("chan", "elem"), "beam"),
        check_vma=False,
    )
```

```python
import functools
import math

import jax
import jax.numpy as jnp
from jax import lax
from jax.experimental import pallas as pl
from jax.experimental.pallas import tpu as pltpu
from jax.sharding import PartitionSpec as P

F32 = jnp.float32
BF16 = jnp.bfloat16
VMEM_BYTES = 40 * 2**20
WINDOW = (2,)
Y_LAG, X_LAG, RING_LAG, UNGATED = 2, 3, 0, 1
FLOPS = 0
TAIL_GATE = 3
TABLE_SLOT = 1
SKEW, SPLIT_SWAPS = 1, 1
CUTS = 2
GROUP = 4
PLAN = ((0, 4), (0, 4), (0, 4), (0, 4), (0, 4), (0, 4), (0, 4), (0, 2), (0, 2))


def groups_of_channels(channels):
    unit = channels // 32
    plan, first = [], 0
    for gathered, units in PLAN:
        plan.append((gathered, first, units * unit))
        first += units * unit
    return plan


def beamform_kernel(sizes, scalars, *refs):
    n, group, time, own, elems, chans, counts, slots = sizes
    halves, refs = refs[: 2 * CUTS], refs[2 * CUTS :]
    blocks, outs = refs[: len(counts)], refs[len(counts) : len(counts) + elems]
    volt, result = refs[len(counts) + elems :]
    step = pl.program_id(0)
    lanes = result.shape[2]
    for g in range(group):
        if blocks[0].shape[2] == time:
            held = blocks[0][:, g].reshape(2 * time, blocks[0].shape[3])
        else:
            slot = 0
            for ref, count in zip(blocks, counts):
                rows = ref.shape[2]
                for j in range(count):
                    at = pl.multiple_of(scalars[slot], rows)
                    volt[g, pl.ds(at, rows), :] = ref[2 * j, g]
                    volt[g, pl.ds(pl.multiple_of(time + at, rows), rows), :] = ref[2 * j + 1, g]
                    slot += 1
            held = volt[g]
        products = []
        for part in range(2):
            total = None
            for j, ref in enumerate(halves[part * CUTS : (part + 1) * CUTS]):
                depth = ref.shape[2]
                term = jnp.dot(held[:, j * depth : (j + 1) * depth], ref[0, g], preferred_element_type=F32)
                total = term if total is None else total + term
            products.append(total)
        by_real, by_imag = products
        real_part = by_real[:time] - by_imag[time:]
        imag_part = by_real[time:] + by_imag[:time]
        row = step * group + g
        for k in range(result.shape[0]):
            cut = slice(k * lanes, (k + 1) * lanes)
            result[k, pl.ds(row, time, stride=2 * n), :] = real_part[:, cut]
            result[k, pl.ds(n + row, time, stride=2 * n), :] = imag_part[:, cut]

    @pl.when(step == n // group - 1)
    def _():
        for r in range(elems):
            for q in range(chans):
                first = pl.multiple_of(scalars[slots + r * chans + q], own) * (2 * n)
                for k in range(result.shape[0]):
                    piece = result[k, pl.ds(pl.multiple_of(first, own * 2 * n), own * 2 * n), :]
                    outs[r][q, :, :, k * lanes : (k + 1) * lanes] = piece.reshape(own, 2 * n, lanes).astype(BF16)


def beamform(scalars, weights, first, n, sources, time, own, elems, chans):
    _, _, depth, beams = weights.shape
    counts = [count for _, count, _ in sources]
    group = math.gcd(math.gcd(first, n), GROUP if n >= 2 * GROUP else GROUP // 2)
    in_specs = [
        pl.BlockSpec(
            (1, group, depth // CUTS, beams), lambda i, s, part=part, j=j: (part, first // group + i, j, 0)
        )
        for part in range(2)
        for j in range(CUTS)
    ]
    for array, count, whole in sources:
        start = first if whole else 0
        in_specs.append(
            pl.BlockSpec((2 * count, group) + array.shape[2:], lambda i, s, start=start: (0, start // group + i, 0, 0))
        )
    shape = (chans, own, 2 * n, beams)
    lanes = min(128, beams)
    return pl.pallas_call(
        functools.partial(beamform_kernel, (n, group, time, own, elems, chans, counts, scalars.shape[0] - elems * chans)),
        out_shape=[jax.ShapeDtypeStruct(shape, BF16)] * elems,
        grid_spec=pltpu.PrefetchScalarGridSpec(
            num_scalar_prefetch=1,
            grid=(n // group,),
            in_specs=in_specs,
            out_specs=[pl.BlockSpec(shape, lambda i, s: (0, 0, 0, 0))] * elems,
            scratch_shapes=[
                pltpu.VMEM((group, 2 * time, depth), BF16),
                pltpu.VMEM((beams // lanes, time * 2 * n, lanes), F32),
            ],
        ),
        compiler_params=pltpu.CompilerParams(vmem_limit_bytes=VMEM_BYTES),
        cost_estimate=pl.CostEstimate(
            flops=FLOPS * n * time * depth * beams,
            bytes_accessed=FLOPS * n * (depth * beams + time * depth + time * beams) // 8,
            transcendentals=0,
        ),
        name="beamform",
    )(scalars, *[weights] * (2 * CUTS), *[array for array, _, _ in sources])


def synthesis_kernel(layout, channels, table, *refs):
    out = refs[-1]
    times, beams = out.shape[1], out.shape[2]
    flat = out.reshape(channels * times, beams)
    lanes = min(128, beams)
    for t in range(times):
        rows, at = [], 0
        for elems, chans in layout:
            total = refs[at][0, t].astype(F32)
            for r in range(1, elems):
                total += refs[at + r][0, t].astype(F32)
            rows.append(total)
            at += elems
            for _ in range(1, chans):
                rows.append(refs[at][t].astype(F32))
                at += 1
        held = jnp.concatenate(rows, axis=0).astype(BF16)
        parts = jnp.dot(table[...], held, preferred_element_type=F32)
        half = 2 * channels
        fine = parts[:half] + (parts[half : 2 * half] + parts[2 * half :])
        out[:, t, :] = fine[:channels] * fine[:channels] + fine[channels:] * fine[channels:]


def synthesis(table, groups, channels, own, beams):
    times = 8
    in_specs = [pl.BlockSpec(table.shape, lambda i: (0, 0))]
    operands, layout = [], []
    for partials, received in groups:
        rows = partials[0].shape[2]
        layout.append((len(partials), 1 + len(received)))
        in_specs += [pl.BlockSpec((1, times, rows, beams), lambda i: (0, i, 0, 0))] * len(partials)
        in_specs += [pl.BlockSpec((times, rows, beams), lambda i: (i, 0, 0))] * len(received)
        operands += list(partials) + list(received)
    return pl.pallas_call(
        functools.partial(synthesis_kernel, layout, channels),
        out_shape=jax.ShapeDtypeStruct((channels, own, beams), F32),
        grid=(own // times,),
        in_specs=in_specs,
        out_specs=pl.BlockSpec((channels, times, beams), lambda i: (0, i, 0)),
        compiler_params=pltpu.CompilerParams(vmem_limit_bytes=VMEM_BYTES),
        cost_estimate=pl.CostEstimate(
            flops=24 * channels * channels * own * beams,
            bytes_accessed=channels * own * beams * 12,
            transcendentals=0,
        ),
        name="synthesis",
    )(table, *operands)


def synthesis_table(channels, local, plan, my_chan, chans):
    places, is_imag = [], []
    for _, first, n in plan:
        for q in range(chans):
            base = lax.rem(my_chan + chans - q, chans) * local + first
            place = base + jnp.arange(n, dtype=jnp.int32)
            places += [place, place]
            is_imag += [False] * n + [True] * n
    column = jnp.concatenate(places)
    imag = jnp.array(is_imag)
    index = jnp.arange(channels, dtype=jnp.int32)
    phase = index[:, None] * column[None, :] % channels
    angle = phase.astype(F32) * (2.0 * jnp.pi / channels)
    factor = 1.0 / jnp.sqrt(F32(channels))
    cosine, sine = jnp.cos(angle) * factor, jnp.sin(angle) * factor
    table = jnp.concatenate([jnp.where(imag, -sine, cosine), jnp.where(imag, cosine, sine)])
    high = lax.reduce_precision(table, 8, 7)
    middle = lax.reduce_precision(table - high, 8, 7)
    low = table - high - middle
    return jnp.concatenate([high, middle, low]).astype(BF16)


def after(value, other):
    return lax.optimization_barrier((value, other))[0]


def shards(voltages, weights):
    local, rows = voltages.shape[1], voltages.shape[2]
    beams = weights.shape[3]
    chans, elems, beam_devices = lax.axis_size("chan"), lax.axis_size("elem"), lax.axis_size("beam")
    channels, time = local * chans, rows * beam_devices
    own = time // (chans * elems)
    cores = 2 if beam_devices % 2 == 0 else 1
    chips = beam_devices // cores
    my_chan, my_elem, my_beam = (lax.axis_index(a) for a in ("chan", "elem", "beam"))
    my_chip, my_core = my_beam // cores, my_beam % cores

    ring = [(d, (d + cores) % beam_devices) for d in range(beam_devices)]
    pair = [(d, d ^ 1) for d in range(beam_devices)]
    plan = groups_of_channels(local)

    mate = lax.ppermute(voltages, "beam", pair) if cores == 2 else None
    table = synthesis_table(channels, local, plan, my_chan, chans)

    def offsets(core):
        return [(lax.rem(my_chip + chips - h, chips) * cores + core) * rows for h in range(chips)]

    mine, others = offsets(my_core), offsets(cores - 1 - my_core)
    piece_starts = [
        (lax.rem(my_chan + q, chans) * elems + lax.rem(my_elem + r, elems)) * own
        for r in range(elems)
        for q in range(chans)
    ]
    places = mine + (others if cores == 2 else [])
    scalars = jnp.stack(places + piece_starts).astype(jnp.int32)

    def partial_beams(k, ahead):
        gathered, first, n = plan[k]
        if gathered:
            sources = [(held[k][1], 1, False)]
        else:
            sources = [(voltages, 1, True)] + [(block, 1, False) for block in held[k][1:]]
            if cores == 2:
                sources.append((mate, 1, True))
                blocks = held[k][1:]
            if k >= 1 and k >= len(plan) - TAIL_GATE:
                blocks = blocks[:-1] + [after(blocks[-1], partials[k - 1][-1])]
            if k < len(plan) - SPLIT_SWAPS:
                early = blocks[:-1]
                sources.append((lax.ppermute(jnp.concatenate(early), "beam", pair), len(early), False))
                blocks = blocks[-1:]
            sources += [(lax.ppermute(block, "beam", pair), 1, False) for block in blocks]
        offsets_now = after(scalars, ahead) if ahead else scalars
        return beamform(offsets_now, weights, first, n, sources, time, own, elems, chans)

    def over_elements(partials):
        moved = [
            lax.ppermute(partials[r], "elem", [(d, (d + r) % elems) for d in range(elems)]) for r in range(1, elems)
        ]
        return [partials[0]] + moved

    def sums_to_send(arrived):
        totals = []
        for q in range(1, chans):
            total = arrived[0][q].astype(F32)
            for part in arrived[1:]:
                total = total + part[q].astype(F32)
            totals.append(total.astype(BF16))
        return totals

    def over_channels(totals):
        return [
            lax.ppermute(total, "chan", [(d, (d + q) % chans) for d in range(chans)])
            for q, total in enumerate(totals, 1)
        ]

    ringed = [k for k in range(len(plan)) if not plan[k][0]]
    lead = ringed[0]
    lead_piece = voltages[:, plan[lead][1] : plan[lead][1] + plan[lead][2]]
    later_pieces = after(voltages, lead_piece)
    held = [[later_pieces[:, first : first + n]] for _, first, n in plan]
    held[lead] = [lead_piece]
    for k, (gathered, _, _) in enumerate(plan):
        if gathered:
            held[k].append(lax.all_gather(held[k][0], "beam", axis=2, tiled=True))
    sent, arrived, received = [], [], []
    count = len(ringed)
    partials = []

    def work_on(k):
        ahead = []
        if k < len(plan) - UNGATED:
            if k >= Y_LAG:
                ahead += arrived[k - Y_LAG][1:]
            if k >= X_LAG:
                ahead += received[k - X_LAG]
        partials.append(partial_beams(k, ahead))
        arrived.append(over_elements(partials[k]))
        received.append(over_channels(sums_to_send(arrived[k])))

    depth = SKEW * (chips - 2) + 1
    for slot in range(count + depth + RING_LAG + 1):
        waits = []
        if 0 <= slot - depth - 1 < count:
            work_on(slot - depth - 1)
        if 0 <= slot - depth - 1 - RING_LAG < count:
            waits.append(partials[slot - depth - 1 - RING_LAG][-1])
        if slot == TABLE_SLOT:
            waits.append(table)
        for h in range(chips - 1):
            k = slot - SKEW * h
            if not 0 <= k < count:
                continue
            block = held[ringed[k]][h]
            ahead = list(waits) + [sent[-w] for w in WINDOW if len(sent) >= w]
            if ahead:
                block = after(block, ahead)
            got = lax.ppermute(block, "beam", ring)
            held[ringed[k]].append(got)
            sent.append(got)

    groups = [(arrived[k], received[k]) for k in range(len(plan))]
    return synthesis(table, groups, channels, own, beams)


def solution(mesh):
    placed = (P(None, "chan", "beam", "elem"), P(None, "chan", "elem", "beam"))
    return jax.shard_map(
        shards,
        mesh=mesh,
        in_specs=placed,
        out_specs=P(None, ("chan", "elem"), "beam"),
        check_vma=False,
    )
```

```python
import functools
import math

import jax
import jax.numpy as jnp
from jax import lax
from jax.experimental import pallas as pl
from jax.experimental.pallas import tpu as pltpu
from jax.sharding import PartitionSpec as P

F32 = jnp.float32
BF16 = jnp.bfloat16
VMEM_BYTES = 40 * 2**20
WINDOW = (2,)
Y_LAG, X_LAG, RING_LAG, UNGATED = 2, 2, 0, 1
FLOPS = 0
TAIL_GATE = 3
TABLE_SLOT = 1
FREE = 0
SKEW, SPLIT_SWAPS = 1, 1
CUTS = 2
GROUP = 4
PLAN = ((0, 4), (0, 4), (0, 4), (0, 4), (0, 4), (0, 4), (0, 4), (0, 2), (0, 2))


def groups_of_channels(channels):
    unit = channels // 32
    plan, first = [], 0
    for gathered, units in PLAN:
        plan.append((gathered, first, units * unit))
        first += units * unit
    return plan


def beamform_kernel(sizes, scalars, *refs):
    n, group, time, own, elems, chans, counts, slots = sizes
    halves, refs = refs[: 2 * CUTS], refs[2 * CUTS :]
    blocks, outs = refs[: len(counts)], refs[len(counts) : len(counts) + elems]
    volt, result = refs[len(counts) + elems :]
    step = pl.program_id(0)
    lanes = result.shape[2]
    for g in range(group):
        if blocks[0].shape[2] == time:
            held = blocks[0][:, g].reshape(2 * time, blocks[0].shape[3])
        else:
            slot = 0
            for ref, count in zip(blocks, counts):
                rows = ref.shape[2]
                for j in range(count):
                    at = pl.multiple_of(scalars[slot], rows)
                    volt[g, pl.ds(at, rows), :] = ref[2 * j, g]
                    volt[g, pl.ds(pl.multiple_of(time + at, rows), rows), :] = ref[2 * j + 1, g]
                    slot += 1
            held = volt[g]
        products = []
        for part in range(2):
            total = None
            for j, ref in enumerate(halves[part * CUTS : (part + 1) * CUTS]):
                depth = ref.shape[2]
                term = jnp.dot(held[:, j * depth : (j + 1) * depth], ref[0, g], preferred_element_type=F32)
                total = term if total is None else total + term
            products.append(total)
        by_real, by_imag = products
        real_part = by_real[:time] - by_imag[time:]
        imag_part = by_real[time:] + by_imag[:time]
        row = step * group + g
        for k in range(result.shape[0]):
            cut = slice(k * lanes, (k + 1) * lanes)
            result[k, pl.ds(row, time, stride=2 * n), :] = real_part[:, cut]
            result[k, pl.ds(n + row, time, stride=2 * n), :] = imag_part[:, cut]

    @pl.when(step == n // group - 1)
    def _():
        for r in range(elems):
            for q in range(chans):
                first = pl.multiple_of(scalars[slots + r * chans + q], own) * (2 * n)
                for k in range(result.shape[0]):
                    piece = result[k, pl.ds(pl.multiple_of(first, own * 2 * n), own * 2 * n), :]
                    outs[r][q, :, :, k * lanes : (k + 1) * lanes] = piece.reshape(own, 2 * n, lanes).astype(BF16)


def beamform(scalars, weights, first, n, sources, time, own, elems, chans):
    _, _, depth, beams = weights.shape
    counts = [count for _, count, _ in sources]
    group = math.gcd(math.gcd(first, n), GROUP if n >= 2 * GROUP else GROUP // 2)
    in_specs = [
        pl.BlockSpec(
            (1, group, depth // CUTS, beams), lambda i, s, part=part, j=j: (part, first // group + i, j, 0)
        )
        for part in range(2)
        for j in range(CUTS)
    ]
    for array, count, whole in sources:
        start = first if whole else 0
        in_specs.append(
            pl.BlockSpec((2 * count, group) + array.shape[2:], lambda i, s, start=start: (0, start // group + i, 0, 0))
        )
    shape = (chans, own, 2 * n, beams)
    lanes = min(128, beams)
    return pl.pallas_call(
        functools.partial(beamform_kernel, (n, group, time, own, elems, chans, counts, scalars.shape[0] - elems * chans)),
        out_shape=[jax.ShapeDtypeStruct(shape, BF16)] * elems,
        grid_spec=pltpu.PrefetchScalarGridSpec(
            num_scalar_prefetch=1,
            grid=(n // group,),
            in_specs=in_specs,
            out_specs=[pl.BlockSpec(shape, lambda i, s: (0, 0, 0, 0))] * elems,
            scratch_shapes=[
                pltpu.VMEM((group, 2 * time, depth), BF16),
                pltpu.VMEM((beams // lanes, (time + 1) * 2 * n, lanes), F32),
            ],
        ),
        compiler_params=pltpu.CompilerParams(vmem_limit_bytes=VMEM_BYTES),
        cost_estimate=pl.CostEstimate(
            flops=FLOPS * n * time * depth * beams,
            bytes_accessed=FLOPS * n * (depth * beams + time * depth + time * beams) // 8,
            transcendentals=0,
        ),
        name="beamform",
    )(scalars, *[weights] * (2 * CUTS), *[array for array, _, _ in sources])


def synthesis_kernel(layout, channels, table, *refs):
    out, rows_of = refs[-2:]
    times, beams = out.shape[1], out.shape[2]
    lanes = min(128, beams)
    for t in range(times):
        rows, at = [], 0
        for elems, chans in layout:
            total = refs[at][0, t].astype(F32)
            for r in range(1, elems):
                total += refs[at + r][0, t].astype(F32)
            rows.append(total)
            at += elems
            for _ in range(1, chans):
                rows.append(refs[at][t].astype(F32))
                at += 1
        held = jnp.concatenate(rows, axis=0).astype(BF16)
        parts = jnp.dot(table[...], held, preferred_element_type=F32)
        half = 2 * channels
        fine = parts[:half] + (parts[half : 2 * half] + parts[2 * half :])
        power = fine[:channels] * fine[:channels] + fine[channels:] * fine[channels:]
        for j in range(beams // lanes):
            rows_of[j, pl.ds(t, channels, stride=times), :] = power[:, j * lanes : (j + 1) * lanes]
    for j in range(beams // lanes):
        out[:, :, j * lanes : (j + 1) * lanes] = rows_of[j, : channels * times].reshape(channels, times, lanes)


def synthesis(table, groups, channels, own, beams):
    times = 8
    in_specs = [pl.BlockSpec(table.shape, lambda i: (0, 0))]
    operands, layout = [], []
    for partials, received in groups:
        rows = partials[0].shape[2]
        layout.append((len(partials), 1 + len(received)))
        in_specs += [pl.BlockSpec((1, times, rows, beams), lambda i: (0, i, 0, 0))] * len(partials)
        in_specs += [pl.BlockSpec((times, rows, beams), lambda i: (i, 0, 0))] * len(received)
        operands += list(partials) + list(received)
    return pl.pallas_call(
        functools.partial(synthesis_kernel, layout, channels),
        out_shape=jax.ShapeDtypeStruct((channels, own, beams), F32),
        grid=(own // times,),
        in_specs=in_specs,
        out_specs=pl.BlockSpec((channels, times, beams), lambda i: (0, i, 0)),
        scratch_shapes=[pltpu.VMEM((beams // min(128, beams), (channels + 1) * times, min(128, beams)), F32)],
        compiler_params=pltpu.CompilerParams(vmem_limit_bytes=VMEM_BYTES),
        cost_estimate=pl.CostEstimate(
            flops=24 * channels * channels * own * beams,
            bytes_accessed=channels * own * beams * 12,
            transcendentals=0,
        ),
        name="synthesis",
    )(table, *operands)


def synthesis_table(channels, local, plan, my_chan, chans):
    places, is_imag = [], []
    for _, first, n in plan:
        for q in range(chans):
            base = lax.rem(my_chan + chans - q, chans) * local + first
            place = base + jnp.arange(n, dtype=jnp.int32)
            places += [place, place]
            is_imag += [False] * n + [True] * n
    column = jnp.concatenate(places)
    imag = jnp.array(is_imag)
    index = jnp.arange(channels, dtype=jnp.int32)
    phase = index[:, None] * column[None, :] % channels
    angle = phase.astype(F32) * (2.0 * jnp.pi / channels)
    factor = 1.0 / jnp.sqrt(F32(channels))
    cosine, sine = jnp.cos(angle) * factor, jnp.sin(angle) * factor
    table = jnp.concatenate([jnp.where(imag, -sine, cosine), jnp.where(imag, cosine, sine)])
    high = lax.reduce_precision(table, 8, 7)
    middle = lax.reduce_precision(table - high, 8, 7)
    low = table - high - middle
    return jnp.concatenate([high, middle, low]).astype(BF16)


def after(value, other):
    return lax.optimization_barrier((value, other))[0]


def shards(voltages, weights):
    local, rows = voltages.shape[1], voltages.shape[2]
    beams = weights.shape[3]
    chans, elems, beam_devices = lax.axis_size("chan"), lax.axis_size("elem"), lax.axis_size("beam")
    channels, time = local * chans, rows * beam_devices
    own = time // (chans * elems)
    cores = 2 if beam_devices % 2 == 0 else 1
    chips = beam_devices // cores
    my_chan, my_elem, my_beam = (lax.axis_index(a) for a in ("chan", "elem", "beam"))
    my_chip, my_core = my_beam // cores, my_beam % cores

    ring = [(d, (d + cores) % beam_devices) for d in range(beam_devices)]
    pair = [(d, d ^ 1) for d in range(beam_devices)]
    plan = groups_of_channels(local)

    mate = lax.ppermute(voltages, "beam", pair) if cores == 2 else None
    table = synthesis_table(channels, local, plan, my_chan, chans)

    def offsets(core):
        return [(lax.rem(my_chip + chips - h, chips) * cores + core) * rows for h in range(chips)]

    mine, others = offsets(my_core), offsets(cores - 1 - my_core)
    piece_starts = [
        (lax.rem(my_chan + q, chans) * elems + lax.rem(my_elem + r, elems)) * own
        for r in range(elems)
        for q in range(chans)
    ]
    places = mine + (others if cores == 2 else [])
    scalars = jnp.stack(places + piece_starts).astype(jnp.int32)

    def partial_beams(k, ahead):
        gathered, first, n = plan[k]
        if gathered:
            sources = [(held[k][1], 1, False)]
        else:
            sources = [(voltages, 1, True)] + [(block, 1, False) for block in held[k][1:]]
            if cores == 2:
                sources.append((mate, 1, True))
                blocks = held[k][1:]
            if k >= 1 and k >= len(plan) - TAIL_GATE:
                blocks = blocks[:-1] + [after(blocks[-1], partials[k - 1][-1])]
            if k < len(plan) - SPLIT_SWAPS:
                early = blocks[:-1]
                sources.append((lax.ppermute(jnp.concatenate(early), "beam", pair), len(early), False))
                blocks = blocks[-1:]
            sources += [(lax.ppermute(block, "beam", pair), 1, False) for block in blocks]
        offsets_now = after(scalars, ahead) if ahead else scalars
        return beamform(offsets_now, weights, first, n, sources, time, own, elems, chans)

    def over_elements(partials):
        moved = [
            lax.ppermute(partials[r], "elem", [(d, (d + r) % elems) for d in range(elems)]) for r in range(1, elems)
        ]
        return [partials[0]] + moved

    def sums_to_send(arrived):
        totals = []
        for q in range(1, chans):
            total = arrived[0][q].astype(F32)
            for part in arrived[1:]:
                total = total + part[q].astype(F32)
            totals.append(total.astype(BF16))
        return totals

    def over_channels(totals):
        return [
            lax.ppermute(total, "chan", [(d, (d + q) % chans) for d in range(chans)])
            for q, total in enumerate(totals, 1)
        ]

    ringed = [k for k in range(len(plan)) if not plan[k][0]]
    lead = ringed[0]
    lead_piece = voltages[:, plan[lead][1] : plan[lead][1] + plan[lead][2]]
    later_pieces = after(voltages, lead_piece)
    held = [[later_pieces[:, first : first + n]] for _, first, n in plan]
    held[lead] = [lead_piece]
    for k, (gathered, _, _) in enumerate(plan):
        if gathered:
            held[k].append(lax.all_gather(held[k][0], "beam", axis=2, tiled=True))
    sent, arrived, received = [], [], []
    count = len(ringed)
    partials = []

    def work_on(k):
        ahead = []
        if k < len(plan) - UNGATED:
            if k >= Y_LAG:
                ahead += arrived[k - Y_LAG][1:]
            if k >= X_LAG:
                ahead += received[k - X_LAG]
        partials.append(partial_beams(k, ahead))
        arrived.append(over_elements(partials[k]))
        received.append(over_channels(sums_to_send(arrived[k])))

    depth = SKEW * (chips - 2) + 1
    for slot in range(count + depth + RING_LAG + 1):
        waits = []
        if 0 <= slot - depth - 1 < count:
            work_on(slot - depth - 1)
        if 0 <= slot - depth - 1 - RING_LAG < count - FREE:
            waits.append(partials[slot - depth - 1 - RING_LAG][-1])
        if slot == TABLE_SLOT:
            waits.append(table)
        for h in range(chips - 1):
            k = slot - SKEW * h
            if not 0 <= k < count:
                continue
            block = held[ringed[k]][h]
            ahead = list(waits) + [sent[-w] for w in WINDOW if len(sent) >= w]
            if ahead:
                block = after(block, ahead)
            got = lax.ppermute(block, "beam", ring)
            held[ringed[k]].append(got)
            sent.append(got)

    groups = [(arrived[k], received[k]) for k in range(len(plan))]
    return synthesis(table, groups, channels, own, beams)


def solution(mesh):
    placed = (P(None, "chan", "beam", "elem"), P(None, "chan", "elem", "beam"))
    return jax.shard_map(
        shards,
        mesh=mesh,
        in_specs=placed,
        out_specs=P(None, ("chan", "elem"), "beam"),
        check_vma=False,
    )
```

```python
import functools
import math

import jax
import jax.numpy as jnp
from jax import lax
from jax.experimental import pallas as pl
from jax.experimental.pallas import tpu as pltpu
from jax.sharding import PartitionSpec as P

F32 = jnp.float32
BF16 = jnp.bfloat16
VMEM_BYTES = 40 * 2**20
WINDOW = (2,)
Y_LAG, X_LAG, RING_LAG, UNGATED = 2, 2, 0, 1
FLOPS = 0
TAIL_GATE = 3
TABLE_SLOT = 1
FREE = 0
SKEW, SPLIT_SWAPS = 1, 1
CUTS = 2
GROUP = 4
PLAN = ((0, 4), (0, 4), (0, 4), (0, 4), (0, 4), (0, 4), (0, 4), (0, 2), (0, 2))


def groups_of_channels(channels):
    unit = channels // 32
    plan, first = [], 0
    for gathered, units in PLAN:
        plan.append((gathered, first, units * unit))
        first += units * unit
    return plan


def beamform_kernel(sizes, scalars, *refs):
    n, group, time, own, elems, chans, counts, slots = sizes
    halves, refs = refs[: 2 * CUTS], refs[2 * CUTS :]
    blocks, outs = refs[: len(counts)], refs[len(counts) : len(counts) + elems]
    volt, result = refs[len(counts) + elems :]
    step = pl.program_id(0)
    lanes = result.shape[2]
    for g in range(group):
        if blocks[0].shape[2] == time:
            held = blocks[0][:, g].reshape(2 * time, blocks[0].shape[3])
        else:
            slot = 0
            for ref, count in zip(blocks, counts):
                rows = ref.shape[2]
                for j in range(count):
                    at = pl.multiple_of(scalars[slot], rows)
                    volt[g, pl.ds(at, rows), :] = ref[2 * j, g]
                    volt[g, pl.ds(pl.multiple_of(time + at, rows), rows), :] = ref[2 * j + 1, g]
                    slot += 1
            held = volt[g]
        products = []
        for part in range(2):
            total = None
            for j, ref in enumerate(halves[part * CUTS : (part + 1) * CUTS]):
                depth = ref.shape[2]
                term = jnp.dot(held[:, j * depth : (j + 1) * depth], ref[0, g], preferred_element_type=F32)
                total = term if total is None else total + term
            products.append(total)
        by_real, by_imag = products
        real_part = by_real[:time] - by_imag[time:]
        imag_part = by_real[time:] + by_imag[:time]
        row = step * group + g
        for k in range(result.shape[0]):
            cut = slice(k * lanes, (k + 1) * lanes)
            result[k, pl.ds(row, time, stride=2 * n), :] = real_part[:, cut]
            result[k, pl.ds(n + row, time, stride=2 * n), :] = imag_part[:, cut]

    @pl.when(step == n // group - 1)
    def _():
        for r in range(elems):
            for q in range(chans):
                first = pl.multiple_of(scalars[slots + r * chans + q], own) * (2 * n)
                for k in range(result.shape[0]):
                    piece = result[k, pl.ds(pl.multiple_of(first, own * 2 * n), own * 2 * n), :]
                    outs[r][q, :, :, k * lanes : (k + 1) * lanes] = piece.reshape(own, 2 * n, lanes).astype(BF16)


def beamform(scalars, weights, first, n, sources, time, own, elems, chans):
    _, _, depth, beams = weights.shape
    counts = [count for _, count, _ in sources]
    group = math.gcd(math.gcd(first, n), GROUP if n >= 2 * GROUP else GROUP // 2)
    in_specs = [
        pl.BlockSpec(
            (1, group, depth // CUTS, beams), lambda i, s, part=part, j=j: (part, first // group + i, j, 0)
        )
        for part in range(2)
        for j in range(CUTS)
    ]
    for array, count, whole in sources:
        start = first if whole else 0
        in_specs.append(
            pl.BlockSpec((2 * count, group) + array.shape[2:], lambda i, s, start=start: (0, start // group + i, 0, 0))
        )
    shape = (chans, own, 2 * n, beams)
    lanes = min(128, beams)
    return pl.pallas_call(
        functools.partial(beamform_kernel, (n, group, time, own, elems, chans, counts, scalars.shape[0] - elems * chans)),
        out_shape=[jax.ShapeDtypeStruct(shape, BF16)] * elems,
        grid_spec=pltpu.PrefetchScalarGridSpec(
            num_scalar_prefetch=1,
            grid=(n // group,),
            in_specs=in_specs,
            out_specs=[pl.BlockSpec(shape, lambda i, s: (0, 0, 0, 0))] * elems,
            scratch_shapes=[
                pltpu.VMEM((group, 2 * time, depth), BF16),
                pltpu.VMEM((beams // lanes, (time + 1) * 2 * n, lanes), F32),
            ],
        ),
        compiler_params=pltpu.CompilerParams(vmem_limit_bytes=VMEM_BYTES),
        cost_estimate=pl.CostEstimate(
            flops=FLOPS * n * time * depth * beams,
            bytes_accessed=FLOPS * n * (depth * beams + time * depth + time * beams) // 8,
            transcendentals=0,
        ),
        name="beamform",
    )(scalars, *[weights] * (2 * CUTS), *[array for array, _, _ in sources])


def synthesis_kernel(layout, channels, table, *refs):
    out, rows_of = refs[-2:]
    times, beams = out.shape[1], out.shape[2]
    lanes = min(128, beams)
    for t in range(times):
        rows, at = [], 0
        for elems, chans in layout:
            total = refs[at][0, t].astype(F32)
            for r in range(1, elems):
                total += refs[at + r][0, t].astype(F32)
            rows.append(total)
            at += elems
            for _ in range(1, chans):
                rows.append(refs[at][t].astype(F32))
                at += 1
        held = jnp.concatenate(rows, axis=0).astype(BF16)
        parts = jnp.dot(table[...], held, preferred_element_type=F32)
        half = 2 * channels
        fine = parts[:half] + (parts[half : 2 * half] + parts[2 * half :])
        power = fine[:channels] * fine[:channels] + fine[channels:] * fine[channels:]
        for j in range(beams // lanes):
            rows_of[j, pl.ds(t, channels, stride=times), :] = power[:, j * lanes : (j + 1) * lanes]
    for j in range(beams // lanes):
        out[:, :, j * lanes : (j + 1) * lanes] = rows_of[j, : channels * times].reshape(channels, times, lanes)


def synthesis(table, groups, channels, own, beams):
    times = 16 if own % 16 == 0 else 8
    in_specs = [pl.BlockSpec(table.shape, lambda i: (0, 0))]
    operands, layout = [], []
    for partials, received in groups:
        rows = partials[0].shape[2]
        layout.append((len(partials), 1 + len(received)))
        in_specs += [pl.BlockSpec((1, times, rows, beams), lambda i: (0, i, 0, 0))] * len(partials)
        in_specs += [pl.BlockSpec((times, rows, beams), lambda i: (i, 0, 0))] * len(received)
        operands += list(partials) + list(received)
    return pl.pallas_call(
        functools.partial(synthesis_kernel, layout, channels),
        out_shape=jax.ShapeDtypeStruct((channels, own, beams), F32),
        grid=(own // times,),
        in_specs=in_specs,
        out_specs=pl.BlockSpec((channels, times, beams), lambda i: (0, i, 0)),
        scratch_shapes=[pltpu.VMEM((beams // min(128, beams), (channels + 1) * times, min(128, beams)), F32)],
        compiler_params=pltpu.CompilerParams(vmem_limit_bytes=VMEM_BYTES),
        cost_estimate=pl.CostEstimate(
            flops=24 * channels * channels * own * beams,
            bytes_accessed=channels * own * beams * 12,
            transcendentals=0,
        ),
        name="synthesis",
    )(table, *operands)


def synthesis_table(channels, local, plan, my_chan, chans):
    places, is_imag = [], []
    for _, first, n in plan:
        for q in range(chans):
            base = lax.rem(my_chan + chans - q, chans) * local + first
            place = base + jnp.arange(n, dtype=jnp.int32)
            places += [place, place]
            is_imag += [False] * n + [True] * n
    column = jnp.concatenate(places)
    imag = jnp.array(is_imag)
    index = jnp.arange(channels, dtype=jnp.int32)
    phase = index[:, None] * column[None, :] % channels
    angle = phase.astype(F32) * (2.0 * jnp.pi / channels)
    factor = 1.0 / jnp.sqrt(F32(channels))
    cosine, sine = jnp.cos(angle) * factor, jnp.sin(angle) * factor
    table = jnp.concatenate([jnp.where(imag, -sine, cosine), jnp.where(imag, cosine, sine)])
    high = lax.reduce_precision(table, 8, 7)
    middle = lax.reduce_precision(table - high, 8, 7)
    low = table - high - middle
    return jnp.concatenate([high, middle, low]).astype(BF16)


def after(value, other):
    return lax.optimization_barrier((value, other))[0]


def shards(voltages, weights):
    local, rows = voltages.shape[1], voltages.shape[2]
    beams = weights.shape[3]
    chans, elems, beam_devices = lax.axis_size("chan"), lax.axis_size("elem"), lax.axis_size("beam")
    channels, time = local * chans, rows * beam_devices
    own = time // (chans * elems)
    cores = 2 if beam_devices % 2 == 0 else 1
    chips = beam_devices // cores
    my_chan, my_elem, my_beam = (lax.axis_index(a) for a in ("chan", "elem", "beam"))
    my_chip, my_core = my_beam // cores, my_beam % cores

    ring = [(d, (d + cores) % beam_devices) for d in range(beam_devices)]
    pair = [(d, d ^ 1) for d in range(beam_devices)]
    plan = groups_of_channels(local)

    mate = lax.ppermute(voltages, "beam", pair) if cores == 2 else None
    table = synthesis_table(channels, local, plan, my_chan, chans)

    def offsets(core):
        return [(lax.rem(my_chip + chips - h, chips) * cores + core) * rows for h in range(chips)]

    mine, others = offsets(my_core), offsets(cores - 1 - my_core)
    piece_starts = [
        (lax.rem(my_chan + q, chans) * elems + lax.rem(my_elem + r, elems)) * own
        for r in range(elems)
        for q in range(chans)
    ]
    places = mine + (others if cores == 2 else [])
    scalars = jnp.stack(places + piece_starts).astype(jnp.int32)

    def partial_beams(k, ahead):
        gathered, first, n = plan[k]
        if gathered:
            sources = [(held[k][1], 1, False)]
        else:
            sources = [(voltages, 1, True)] + [(block, 1, False) for block in held[k][1:]]
            if cores == 2:
                sources.append((mate, 1, True))
                blocks = held[k][1:]
            if k >= 1 and k >= len(plan) - TAIL_GATE:
                blocks = blocks[:-1] + [after(blocks[-1], partials[k - 1][-1])]
            if k < len(plan) - SPLIT_SWAPS:
                early = blocks[:-1]
                sources.append((lax.ppermute(jnp.concatenate(early), "beam", pair), len(early), False))
                blocks = blocks[-1:]
            sources += [(lax.ppermute(block, "beam", pair), 1, False) for block in blocks]
        offsets_now = after(scalars, ahead) if ahead else scalars
        return beamform(offsets_now, weights, first, n, sources, time, own, elems, chans)

    def over_elements(partials):
        moved = [
            lax.ppermute(partials[r], "elem", [(d, (d + r) % elems) for d in range(elems)]) for r in range(1, elems)
        ]
        return [partials[0]] + moved

    def sums_to_send(arrived):
        totals = []
        for q in range(1, chans):
            total = arrived[0][q].astype(F32)
            for part in arrived[1:]:
                total = total + part[q].astype(F32)
            totals.append(total.astype(BF16))
        return totals

    def over_channels(totals):
        return [
            lax.ppermute(total, "chan", [(d, (d + q) % chans) for d in range(chans)])
            for q, total in enumerate(totals, 1)
        ]

    ringed = [k for k in range(len(plan)) if not plan[k][0]]
    lead = ringed[0]
    lead_piece = voltages[:, plan[lead][1] : plan[lead][1] + plan[lead][2]]
    later_pieces = after(voltages, lead_piece)
    held = [[later_pieces[:, first : first + n]] for _, first, n in plan]
    held[lead] = [lead_piece]
    for k, (gathered, _, _) in enumerate(plan):
        if gathered:
            held[k].append(lax.all_gather(held[k][0], "beam", axis=2, tiled=True))
    sent, arrived, received = [], [], []
    count = len(ringed)
    partials = []

    def work_on(k):
        ahead = []
        if k < len(plan) - UNGATED:
            if k >= Y_LAG:
                ahead += arrived[k - Y_LAG][1:]
            if k >= X_LAG:
                ahead += received[k - X_LAG]
        partials.append(partial_beams(k, ahead))
        arrived.append(over_elements(partials[k]))
        received.append(over_channels(sums_to_send(arrived[k])))

    depth = SKEW * (chips - 2) + 1
    for slot in range(count + depth + RING_LAG + 1):
        waits = []
        if 0 <= slot - depth - 1 < count:
            work_on(slot - depth - 1)
        if 0 <= slot - depth - 1 - RING_LAG < count - FREE:
            waits.append(partials[slot - depth - 1 - RING_LAG][-1])
        if slot == TABLE_SLOT:
            waits.append(table)
        for h in range(chips - 1):
            k = slot - SKEW * h
            if not 0 <= k < count:
                continue
            block = held[ringed[k]][h]
            ahead = list(waits) + [sent[-w] for w in WINDOW if len(sent) >= w]
            if ahead:
                block = after(block, ahead)
            got = lax.ppermute(block, "beam", ring)
            held[ringed[k]].append(got)
            sent.append(got)

    groups = [(arrived[k], received[k]) for k in range(len(plan))]
    return synthesis(table, groups, channels, own, beams)


def solution(mesh):
    placed = (P(None, "chan", "beam", "elem"), P(None, "chan", "elem", "beam"))
    return jax.shard_map(
        shards,
        mesh=mesh,
        in_specs=placed,
        out_specs=P(None, ("chan", "elem"), "beam"),
        check_vma=False,
    )
```
